512 devices in a mesh: pulse: 32 (over z_hi, y, core), tile: 16 (over x, z_lo).
Axes of the slice: x: 4, y: 8, z: 8 (z_hi: 2, z_lo: 4; z = z_hi * 4 + z_lo), core: 2. Of those that a mesh axis runs over, the one named last changes fastest.
Arguments:
- raw: bfloat16 [8192, 4, 2, 8192], P(('pulse', 'tile')), may hold values from -6 to 6
- chirp: bfloat16 [4, 2, 128], replicated, may hold values from -0.1875 to 0.1875
- steer: float32 [8192, 128], P('pulse'), may hold values from -3.140625 to 3.140625
- offsets: int32 [5, 2, 128], replicated, may hold values from 0 to 124, as said below
- interp: bfloat16 [5, 2, 2, 4, 2, 128], replicated, may hold values from -1.5 to 1.5
- owner: int32 [16], replicated, may hold values from 0 to 15, each once
Outputs:
- image: bfloat16 [2, 4096, 8192], P(None, 'pulse', 'tile')
The draws below stay inside these ranges and needn't reach their ends.
Inputs may be any that keep to these rules, and one draw needn't show every extreme that they name: Each offsets[l, b, a] lies between (b * 128 + a) // 2 - 4 // 2 and (b * 128 + a) // 2 - 4 // 2 + 2, clipped to the range. `owner`: each tile holds a different range block.
All inputs are finite; a program needn't handle non-finite values.
Results may differ from the reference program's by a relative error of at most 0.0084.
Values may be sent and summed in bfloat16 or wider, within the bound.
No kernel may reach another device: no remote copies, remote signals or barrier semaphores. Data moves between devices by JAX's collectives and lax.ppermute only.
A program may use at most 64 MiB of HBM per device.

```python
import jax
import jax.numpy as jnp
from jax import lax

S = 8192
CH = 4
KTAP = 128
A = 128
KB = 4
LEVELS = 5
R = 512
P_G = 256
PULSES = 8192
N_PULSE = 32
N_TILE = 16


def draw_offsets(key, part):
    fine = jnp.arange(A, dtype=jnp.int32)[None, None, :]
    half = jnp.arange(2, dtype=jnp.int32)[None, :, None]
    jitter = jax.random.randint(key, (LEVELS, 2, A), -1, 2, dtype=jnp.int32)
    start = (half * A + fine) // 2 - KB // 2 + 1 + jitter
    return jnp.clip(start, 0, A - KB).astype(jnp.int32)


def block_levels(stream_key, extent, cuts, smallest, high):
    def one(position, blocks):
        draws = jax.random.uniform(jax.random.fold_in(jax.random.fold_in(stream_key, 6), position), (blocks,), jnp.float32, smallest / len(cuts), high / len(cuts))
        return jnp.repeat(jnp.exp(draws), extent[position] // blocks).reshape((-1,) + (1,) * (len(extent) - position - 1))

    gain = one(*cuts[0])
    for cut in cuts[1:]:
        gain = gain * one(*cut)
    return gain


def normal_values(rng, extent, spread, most, cuts=(), kind=jnp.bfloat16):
    entries = jax.random.normal(rng, extent, jnp.float32) * spread
    if len(cuts) > 0:
        entries = block_levels(rng, extent, cuts, -0.22, 0.18) * entries
    return jnp.clip(entries, min=-most, max=most).astype(kind)


def setup_inputs(seed: int = 0) -> dict:
    key_of = jax.random.split(jax.random.key(seed), 7)
    raw = normal_values(key_of[0], (PULSES, CH, 2, S), 1.0, 6.0, ((0, 512),))
    chirp = normal_values(key_of[1], (CH, 2, KTAP), (2 * CH * KTAP) ** -0.5, 0.1875)
    steer = jnp.clip(jax.random.uniform(key_of[2], (PULSES, A), jnp.float32, -3.140625, 3.140625), -3.140625, 3.140625)
    offsets = draw_offsets(jax.random.fold_in(key_of[6], 71), 0)
    interp = normal_values(key_of[4], (LEVELS, 2, 2, KB, 2, A), (4 * KB) ** -0.5, 1.5)
    owner = jax.random.permutation(key_of[5], N_TILE).astype(jnp.int32)
    return dict(raw=raw, chirp=chirp, steer=steer, offsets=offsets, interp=interp, owner=owner)


def apply_band(img, wk, offs):
    real_acc = jnp.zeros(img.shape[1:], jnp.float32)
    imag_acc = jnp.zeros(img.shape[1:], jnp.float32)
    for tap in range(KB):
        picked = img[:, offs + tap, :]
        w_real = wk[tap, 0][:, None]
        w_imag = wk[tap, 1][:, None]
        real_acc = real_acc + w_real * picked[0] - w_imag * picked[1]
        imag_acc = imag_acc + w_imag * picked[0] + w_real * picked[1]
    return jnp.stack([real_acc, imag_acc])

def reference(raw, chirp, steer, offsets, interp, owner):
    taps = chirp.astype(jnp.float32)
    filt = taps[:, 0] + 1j * taps[:, 1]
    filt_hat = jnp.fft.fft(filt[:, ::-1], n=2 * S, axis=-1)
    scale = 1.0 / jnp.sqrt(jnp.float32(P_G))
    theta = steer.reshape(N_PULSE, P_G, A)
    cos_all = (jnp.cos(theta) * scale).astype(jnp.bfloat16).astype(jnp.float32)
    sin_all = (jnp.sin(theta) * scale).astype(jnp.bfloat16).astype(jnp.float32)

    def group(items):
        samples, cos_part, sin_part = items
        values = samples.astype(jnp.float32)
        signal = values[:, :, 0] + 1j * values[:, :, 1]
        spectrum = jnp.fft.fft(signal, n=2 * S, axis=-1)
        summed = lax.optimization_barrier(jnp.sum(spectrum * filt_hat[None], axis=1))
        full = jnp.fft.ifft(summed, axis=-1)[:, KTAP - 1:KTAP - 1 + S]
        comp_real = jnp.real(full).astype(jnp.bfloat16).astype(jnp.float32)
        comp_imag = jnp.imag(full).astype(jnp.bfloat16).astype(jnp.float32)
        hp = lax.Precision.HIGHEST
        out_real = jnp.einsum('pa,ps->as', cos_part, comp_real, precision=hp) - jnp.einsum('pa,ps->as', sin_part, comp_imag, precision=hp)
        out_imag = jnp.einsum('pa,ps->as', sin_part, comp_real, precision=hp) + jnp.einsum('pa,ps->as', cos_part, comp_imag, precision=hp)
        return jnp.stack([out_real, out_imag]).astype(jnp.bfloat16)
    current = lax.map(group, (raw.reshape(N_PULSE, P_G, CH, 2, S), cos_all, sin_all))
    weights = interp.astype(jnp.float32)
    groups = jnp.arange(N_PULSE, dtype=jnp.int32)
    for level in range(LEVELS):
        bits = groups // 2 ** level % 2
        partner = groups + (1 - 2 * bits) * 2 ** level
        values = current.astype(jnp.float32)
        other = values[partner]
        own_w = weights[level, bits, bits]
        other_w = weights[level, bits, 1 - bits]
        offs = offsets[level, bits]
        merged = jax.vmap(apply_band)(values, own_w, offs) + jax.vmap(apply_band)(other, other_w, offs)
        current = merged.astype(jnp.bfloat16)
    blocks = current.reshape(N_PULSE, 2, A, N_TILE, R)[:, :, :, owner]
    return jnp.transpose(blocks, (1, 0, 2, 3, 4)).reshape(2, N_PULSE * A, N_TILE * R)
```

```python
import functools
import itertools
import math

import jax
import jax.numpy as jnp
import numpy as np
from jax import lax
from jax.experimental import pallas as pl
from jax.experimental.pallas import tpu as pltpu
from jax.sharding import Mesh
from jax.sharding import PartitionSpec as P

S = 8192
CH = 4
KTAP = 128
A = 128
KB = 4
R = 512
P_G = 256
N_TILE = 16
P_HERE = 16
BLOCKS = S // KTAP
PER = R // KTAP
WIN = 20
HALF = 80
N_FAR = 16
F32 = jnp.float32
BF16 = jnp.bfloat16
VMEM = pl.BlockSpec(memory_space=pltpu.VMEM)
SMEM = pl.BlockSpec(memory_space=pltpu.SMEM)


def band_range(half, low, high):
    first = min(max((half * A + low) // 2 - KB // 2, 0), A - KB)
    last = min(max((half * A + high) // 2, 0), A - KB)
    return first, last + KB - 1


def far_window(bits):
    low, high = 0, A - 1
    for half in reversed(bits):
        low, high = band_range(half, low, high)
    return low, high


def far_lows():
    lows = []
    for d in range(N_FAR):
        low, high = far_window([d >> i & 1 for i in range(4)])
        assert high - low + 1 <= WIN
        lows.append(low)
    return lows


def row_pick():
    table = np.zeros((N_FAR, 2, WIN, 2, A), np.float32)
    for d, low in enumerate(far_lows()):
        for part in range(2):
            for i in range(WIN):
                if low + i < A:
                    table[d, part, i, part, low + i] = 1
    return table.reshape(N_FAR * 2 * WIN, 2 * A).astype(jnp.bfloat16)


def order_pick():
    table = np.zeros((2, 8, P_HERE, P_HERE, 8, 2), np.float32)
    for q, b, p in itertools.product(range(2), range(8), range(P_HERE)):
        table[q, b, p, p, b, q] = 1
    return table.reshape(256, 256).astype(jnp.bfloat16)


def compress_kernel(owner_ref, chirp_ref, pick_ref, x_ref, out_ref, inv_ref, table_ref, z_ref):
    for t in range(N_TILE):
        inv_ref[owner_ref[t]] = t
    row = lax.broadcasted_iota(jnp.int32, (KTAP, KTAP), 0)
    col = lax.broadcasted_iota(jnp.int32, (KTAP, KTAP), 1)
    flip = jnp.where((row + col) % KTAP == 0, 1.0, 0.0).astype(BF16)
    half = CH * KTAP
    for c in range(CH):
        taps = chirp_ref[c].astype(F32)
        for q in range(2):
            line = jnp.broadcast_to(taps[q : q + 1], (16, KTAP)).astype(BF16)
            line = jnp.dot(line, flip, preferred_element_type=F32)
            circ = jnp.broadcast_to(line[0:1], (KTAP, KTAP))
            circ = pltpu.roll(circ, 0, 1, stride=1, stride_axis=0)
            for upper in range(2):
                keep = (row < col) if upper else (row >= col)
                kept = jnp.where(keep, circ, 0.0)
                base = upper * 2 * half + c * KTAP
                if q == 0:
                    table_ref[base : base + KTAP, 0:KTAP] = kept.astype(BF16)
                    table_ref[base + half : base + half + KTAP, KTAP:] = kept.astype(BF16)
                else:
                    table_ref[base : base + KTAP, KTAP:] = kept.astype(BF16)
                    table_ref[base + half : base + half + KTAP, 0:KTAP] = (-kept).astype(BF16)
    z_ref[BLOCKS * P_HERE :, :] = jnp.zeros((P_HERE, 2 * half), BF16)
    pick = pick_ref[...]
    for g in range(BLOCKS // 8):
        parts = []
        for c in range(CH):
            got = x_ref[:, c, 16 * g : 16 * g + 16, :]
            parts.append(got.reshape(256, KTAP))
        moved = jnp.dot(pick, jnp.concatenate(parts, axis=1), preferred_element_type=F32)
        moved = moved.astype(BF16)
        z_ref[128 * g : 128 * g + 128, 0:half] = moved[0:128]
        z_ref[128 * g : 128 * g + 128, half:] = moved[128:256]
    for m in range(4):
        lower = z_ref[256 * m : 256 * m + 256, :]
        upper = z_ref[256 * m + 16 : 256 * m + 272, :]
        acc = jnp.dot(lower, table_ref[0 : 2 * half, :], preferred_element_type=F32)
        acc = acc + jnp.dot(upper, table_ref[2 * half :, :], preferred_element_type=F32)
        acc = acc.astype(BF16)
        for n in range(4):
            to = inv_ref[4 * m + n]
            for j in range(PER):
                base = 16 * (PER * n + j)
                for o in range(2):
                    out_ref[to, j, o] = acc[base : base + 16, 128 * o : 128 * o + 128]


def project_kernel(pos_ref, steer_ref, got_ref, send_ref, own_ref, w_ref):
    theta = steer_ref[...]
    scale = 1.0 / math.sqrt(P_G)
    cos_part = (jnp.cos(theta) * scale).astype(BF16).reshape(N_TILE, P_HERE, A)
    sin_part = (jnp.sin(theta) * scale).astype(BF16).reshape(N_TILE, P_HERE, A)
    first = jnp.concatenate([cos_part, sin_part], axis=2)
    second = jnp.concatenate([-sin_part, cos_part], axis=2)
    full = jnp.stack([first, second], axis=1).reshape(2 * P_G, 2 * A)
    w_ref[...] = full.T
    mine = pos_ref[0]
    rows = []
    for half in (1 - mine, mine):
        low = pl.multiple_of(half * (A - HALF), 16)
        rows.append(w_ref[pl.ds(low, HALF), :])
        rows.append(w_ref[pl.ds(pl.multiple_of(A + low, 16), HALF), :])
    weights = jnp.concatenate(rows, axis=0)
    for j in range(PER):
        block = got_ref[:, 32 * j : 32 * j + 32, :].reshape(2 * P_G, KTAP)
        made = jnp.dot(weights, block, preferred_element_type=F32).astype(BF16)
        send_ref[:, 128 * j : 128 * j + 128] = made[: 2 * HALF]
        own_ref[:, 128 * j : 128 * j + 128] = made[2 * HALF :]


def band_t(interp_ref, offsets_ref, level, half, child, low, count):
    both = offsets_ref[level]
    starts = jnp.where(half == 0, both[0:1], both[1:2])
    row = lax.broadcasted_iota(jnp.int32, (count, A), 0) + low
    delta = row - starts
    real = jnp.zeros((count, A), F32)
    imag = jnp.zeros((count, A), F32)
    for k in range(KB):
        taps = interp_ref[level, half, child, k].astype(F32)
        hit = delta == k
        real = jnp.where(hit, taps[0:1], real)
        imag = jnp.where(hit, taps[1:2], imag)
    upper = jnp.concatenate([real, imag], axis=1)
    lower = jnp.concatenate([-imag, real], axis=1)
    return jnp.concatenate([upper, lower], axis=0).astype(BF16)


def tables_kernel(pos_ref, lows_ref, interp_ref, offsets_ref, pick_ref, near_ref, far_ref):
    nt = (((1,), (1,)), ((), ()))
    mine = pos_ref[0]
    d = pos_ref[1]
    low = mine * (A - HALF)
    near = [
        band_t(interp_ref, offsets_ref, 0, mine, mine, low, HALF),
        band_t(interp_ref, offsets_ref, 0, mine, 1 - mine, low, HALF),
    ]
    near = jnp.concatenate(near, axis=0)
    near_ref[...] = lax.dot_general(pick_ref[...], near, nt, preferred_element_type=F32).astype(BF16)
    bits = [d & 1, d // 2 & 1, d // 4 & 1, d // 8 & 1]
    low = lows_ref[d]
    stack = [band_t(interp_ref, offsets_ref, 1, bits[0], q, low, WIN) for q in range(2)]
    chain = jnp.concatenate(stack, axis=0)
    for level in range(2, 5):
        grown = []
        for q in range(2):
            step = band_t(interp_ref, offsets_ref, level, bits[level - 1], q, 0, A)
            grown.append(jnp.dot(chain, step, preferred_element_type=F32).astype(BF16))
        chain = jnp.concatenate(grown, axis=0)
    far_ref[...] = chain.T


def merge_kernel(near_ref, own_ref, other_ref, out_ref):
    data = jnp.concatenate([own_ref[...], other_ref[...]], axis=0)
    made = jnp.dot(near_ref[...], data, preferred_element_type=F32)
    made = made.astype(BF16)
    for d in range(N_FAR):
        for j in range(PER):
            out_ref[d, j] = made[2 * WIN * d : 2 * WIN * d + 2 * WIN, 128 * j : 128 * j + 128]


def final_kernel(far_ref, got_ref, out_ref):
    for j in range(PER):
        block = got_ref[:, j].reshape(N_FAR * 2 * WIN, KTAP)
        made = jnp.dot(far_ref[...], block, preferred_element_type=F32).astype(BF16)
        out_ref[0, :, 128 * j : 128 * j + 128] = made[:A]
        out_ref[1, :, 128 * j : 128 * j + 128] = made[A:]


def call(body, ins, outs, scratch=(), limit=48):
    return pl.pallas_call(
        body,
        out_shape=[jax.ShapeDtypeStruct(shape, BF16) for shape in outs],
        in_specs=ins,
        out_specs=[VMEM] * len(outs),
        scratch_shapes=list(scratch),
        compiler_params=pltpu.CompilerParams(vmem_limit_bytes=limit * 2**20),
    )


def shards(raw, chirp, steer, offsets, interp, owner):
    mine = lax.axis_index("c")
    far = lax.axis_index("h") * 8 + lax.axis_index("y")
    pos = jnp.stack([mine, far]).astype(jnp.int32)
    x = raw.reshape(P_HERE, CH, 2, BLOCKS, KTAP).transpose(0, 1, 3, 2, 4)
    x = x.reshape(P_HERE, CH, 2 * BLOCKS, KTAP)
    (packed,) = call(
        compress_kernel,
        [SMEM, VMEM, VMEM, VMEM],
        [(N_TILE, PER, 2, P_HERE, KTAP)],
        [
            pltpu.SMEM((N_TILE,), jnp.int32),
            pltpu.VMEM((4 * CH * KTAP, 2 * KTAP), BF16),
            pltpu.VMEM(((BLOCKS + 1) * P_HERE, 2 * CH * KTAP), BF16),
        ],
    )(owner, chirp, jnp.asarray(order_pick()), x)
    packed = packed.reshape(N_TILE, PER * 2 * P_HERE, KTAP)
    got = lax.all_to_all(packed, ("x", "l"), 0, 0, tiled=True)
    near, far_table = call(
        tables_kernel,
        [SMEM, SMEM, VMEM, VMEM, VMEM],
        [(N_FAR * 2 * WIN, 4 * HALF), (2 * A, N_FAR * 2 * WIN)],
    )(pos, jnp.asarray(far_lows(), jnp.int32), interp, offsets, jnp.asarray(row_pick()))
    send, own = call(
        project_kernel,
        [SMEM, VMEM, VMEM],
        [(2 * HALF, R), (2 * HALF, R)],
        [pltpu.VMEM((2 * A, 2 * P_G), BF16)],
    )(pos, steer, got)
    other = lax.ppermute(send, "c", [(0, 1), (1, 0)])
    (pieces,) = call(merge_kernel, [VMEM] * 3, [(N_FAR, PER, 2 * WIN, KTAP)])(near, own, other)
    pieces = pieces.reshape(N_FAR, PER * 2 * WIN, KTAP)
    parts = lax.all_to_all(pieces, ("h", "y"), 0, 0, tiled=True)
    parts = parts.reshape(N_FAR, PER, 2 * WIN, KTAP)
    (image,) = call(final_kernel, [VMEM] * 2, [(2, A, R)])(far_table, parts)
    return image


def solution(mesh):
    split = Mesh(mesh.devices.reshape(2, 8, 2, 4, 4), ("h", "y", "c", "x", "l"))
    pulse = ("h", "y", "c")
    tile = ("x", "l")
    placed = (P(pulse + tile, None, None, None), P(), P(pulse, None), P(), P(), P())
    return jax.shard_map(
        shards, mesh=split, in_specs=placed, out_specs=P(None, pulse, tile), check_vma=False
    )
```

```python
import math

import jax
import jax.numpy as jnp
import numpy as np
from jax import lax
from jax.experimental import pallas as pl
from jax.experimental.pallas import tpu as pltpu
from jax.sharding import Mesh
from jax.sharding import PartitionSpec as P

S = 8192
CH = 4
KTAP = 128
A = 128
KB = 4
R = 512
P_G = 256
N_TILE = 16
P_HERE = 16
BLOCKS = S // KTAP
PER = R // KTAP
WIN = 25
MAIN = 48
REST = 4
FAR_ROWS = 56
PIECE = PER * (MAIN + REST)
HALF = 72
N_Y = 8
F32 = jnp.float32
BF16 = jnp.bfloat16
VMEM = pl.BlockSpec(memory_space=pltpu.VMEM)
HBM = pl.BlockSpec(memory_space=pltpu.HBM)


def band_range(half, low, high):
    first = min(max((half * A + low) // 2 - KB // 2, 0), A - KB)
    last = min(max((half * A + high) // 2, 0), A - KB)
    return first, last + KB - 1


def window_lows():
    lows = []
    for y in range(N_Y):
        low, high = 0, A - 1
        for level in (3, 2, 1):
            low, high = band_range(y >> level - 1 & 1, low, high)
        assert high - low + 1 <= WIN
        lows.append(low)
    return lows


def row_pick():
    table = np.zeros((N_Y, MAIN + REST, 2, A), np.float32)
    for y, low in enumerate(window_lows()):
        for part in range(2):
            for i in range(min(WIN, A - low)):
                table[y, part * WIN + i, part, low + i] = 1
    table = table.reshape(N_Y, MAIN + REST, 2 * A)
    first = table[:, :MAIN].reshape(N_Y * MAIN, 2 * A)
    rest = table[:, MAIN:].reshape(N_Y * REST, 2 * A)
    return np.concatenate([first, rest]).astype(jnp.bfloat16)


def one_hot(rows, cols, wanted):
    row = lax.broadcasted_iota(jnp.int32, (rows, cols), 0)
    col = lax.broadcasted_iota(jnp.int32, (rows, cols), 1)
    return jnp.where(wanted(row, col), 1.0, 0.0).astype(BF16)


def compress_kernel(
    owner_hbm, chirp_hbm, x_hbm, out_ref, token_ref, owner_ref, chirp_ref, x_ref, inv_ref, table_ref, z_ref, sem
):
    steps = BLOCKS // 8
    loads = [
        pltpu.make_async_copy(
            x_hbm.at[:, :, 16 * g : 16 * g + 16, :], x_ref.at[:, :, 16 * g : 16 * g + 16, :], sem.at[g]
        )
        for g in range(steps)
    ]
    chirp_load = pltpu.make_async_copy(chirp_hbm, chirp_ref, sem.at[steps])
    owner_load = pltpu.make_async_copy(owner_hbm, owner_ref, sem.at[steps + 1])
    token_ref[...] = jnp.zeros(token_ref.shape, BF16)
    chirp_load.start()
    for load in loads:
        load.start()
    owner_load.start()
    row = lax.broadcasted_iota(jnp.int32, (KTAP, KTAP), 0)
    col = lax.broadcasted_iota(jnp.int32, (KTAP, KTAP), 1)
    flip = jnp.where((row + col) % KTAP == 0, 1.0, 0.0).astype(BF16)
    pick = one_hot(256, 256, lambda r, c: c == r % 16 * 16 + r // 16 % 8 * 2 + r // 128)
    half = CH * KTAP
    z_ref[BLOCKS * P_HERE :, :] = jnp.zeros((P_HERE, 2 * half), BF16)
    chirp_load.wait()
    for c in range(CH):
        taps = chirp_ref[c].astype(F32)
        for q in range(2):
            line = jnp.broadcast_to(taps[q : q + 1], (16, KTAP)).astype(BF16)
            line = jnp.dot(line, flip, preferred_element_type=F32)
            circ = jnp.broadcast_to(line[0:1], (KTAP, KTAP))
            circ = pltpu.roll(circ, 0, 1, stride=1, stride_axis=0)
            for upper in range(2):
                keep = (row < col) if upper else (row >= col)
                kept = jnp.where(keep, circ, 0.0)
                base = upper * 2 * half + c * KTAP
                if q == 0:
                    table_ref[base : base + KTAP, 0:KTAP] = kept.astype(BF16)
                    table_ref[base + half : base + half + KTAP, KTAP:] = kept.astype(BF16)
                else:
                    table_ref[base : base + KTAP, KTAP:] = kept.astype(BF16)
                    table_ref[base + half : base + half + KTAP, 0:KTAP] = (-kept).astype(BF16)
    owner_load.wait()
    for t in range(N_TILE):
        inv_ref[owner_ref[t]] = t
    for g in range(steps):
        loads[g].wait()
        parts = []
        for c in range(CH):
            got = x_ref[:, c, 16 * g : 16 * g + 16, :]
            parts.append(got.reshape(256, KTAP))
        moved = jnp.dot(pick, jnp.concatenate(parts, axis=1), preferred_element_type=F32)
        moved = moved.astype(BF16)
        z_ref[128 * g : 128 * g + 128, 0:half] = moved[0:128]
        z_ref[128 * g : 128 * g + 128, half:] = moved[128:256]
    for m in range(4):
        lower = z_ref[256 * m : 256 * m + 256, :]
        upper = z_ref[256 * m + 16 : 256 * m + 272, :]
        acc = jnp.dot(lower, table_ref[0 : 2 * half, :], preferred_element_type=F32)
        acc = acc + jnp.dot(upper, table_ref[2 * half :, :], preferred_element_type=F32)
        acc = acc.astype(BF16)
        for n in range(4):
            to = inv_ref[4 * m + n]
            for j in range(PER):
                base = 16 * (PER * n + j)
                for o in range(2):
                    out_ref[to, j, o] = acc[base : base + 16, 128 * o : 128 * o + 128]


def band_parts(interp_ref, offsets_ref, level, half, child, rows):
    both = offsets_ref[level]
    starts = jnp.where(half == 0, both[0:1], both[1:2])
    delta = rows - starts
    real = jnp.zeros(rows.shape, F32)
    imag = jnp.zeros(rows.shape, F32)
    for k in range(KB):
        taps = interp_ref[level, half, child, k].astype(F32)
        hit = delta == k
        real = jnp.where(hit, taps[0:1], real)
        imag = jnp.where(hit, taps[1:2], imag)
    return real, imag


def band_t(interp_ref, offsets_ref, level, half, child, low, count):
    rows = lax.broadcasted_iota(jnp.int32, (count, A), 0) + low
    real, imag = band_parts(interp_ref, offsets_ref, level, half, child, rows)
    upper = jnp.concatenate([real, imag], axis=1)
    lower = jnp.concatenate([-imag, real], axis=1)
    return jnp.concatenate([upper, lower], axis=0).astype(BF16)


def prep_kernel(after_ref, steer_ref, interp_ref, offsets_ref, pick_ref, weights_ref, near_ref, w_ref):
    del after_ref
    mine = lax.axis_index("c")
    theta = steer_ref[...]
    scale = 1.0 / math.sqrt(P_G)
    cos_part = (jnp.cos(theta) * scale).astype(BF16).reshape(N_TILE, P_HERE, A)
    sin_part = (jnp.sin(theta) * scale).astype(BF16).reshape(N_TILE, P_HERE, A)
    first = jnp.concatenate([cos_part, sin_part], axis=2)
    second = jnp.concatenate([-sin_part, cos_part], axis=2)
    full = jnp.stack([first, second], axis=1).reshape(2 * P_G, 2 * A)
    w_ref[...] = full.T.astype(F32)
    half_rows(w_ref, weights_ref, mine)
    low = mine * (A - HALF)
    near = [
        band_t(interp_ref, offsets_ref, 0, mine, mine, low, HALF),
        band_t(interp_ref, offsets_ref, 0, mine, 1 - mine, low, HALF),
    ]
    near = jnp.concatenate(near, axis=0)
    nt = (((1,), (1,)), ((), ()))
    near_ref[...] = lax.dot_general(pick_ref[...], near, nt, preferred_element_type=F32).astype(BF16)


def half_rows(full_ref, out_ref, mine):
    for n, side in enumerate((1 - mine, mine)):
        for part in range(2):
            low = pl.multiple_of(part * A + side * (A - HALF), 8)
            at = (2 * n + part) * HALF
            out_ref[at : at + HALF, :] = full_ref[pl.ds(low, HALF), :].astype(BF16)


def project_kernel(weights_ref, got_ref, send_ref, own_ref):
    for j in range(PER):
        block = got_ref[:, 32 * j : 32 * j + 32, :].reshape(2 * P_G, KTAP)
        made = jnp.dot(weights_ref[...], block, preferred_element_type=F32).astype(BF16)
        send_ref[:, 128 * j : 128 * j + 128] = made[: 2 * HALF]
        own_ref[:, 128 * j : 128 * j + 128] = made[2 * HALF :]


def far_kernel(after_ref, interp_ref, offsets_ref, far_ref, full_ref):
    del after_ref
    y = lax.axis_index("y")
    bits = [y & 1, y >> 1 & 1, y >> 2 & 1]
    low = jnp.int32(0)
    for bit in reversed(bits):
        low = jnp.clip((bit * A + low) // 2 - KB // 2, 0, A - KB)
    n = lax.broadcasted_iota(jnp.int32, (FAR_ROWS, A), 0)
    second = n >= WIN
    rows = low + n - jnp.where(second, WIN, 0)
    chain = []
    for q in range(2):
        real, imag = band_parts(interp_ref, offsets_ref, 1, bits[0], q, rows)
        left = jnp.where(second, -imag, real)
        right = jnp.where(second, real, imag)
        chain.append(jnp.concatenate([left, right], axis=1))
    chain = jnp.concatenate(chain, axis=0)
    for level in range(2, 4):
        grown = []
        for q in range(2):
            step = band_t(interp_ref, offsets_ref, level, bits[level - 1], q, 0, A)
            grown.append(jnp.dot(chain.astype(BF16), step, preferred_element_type=F32))
        chain = jnp.concatenate(grown, axis=0)
    chain = chain.reshape(N_Y, FAR_ROWS, 2 * A)
    first = chain[:, :MAIN].reshape(N_Y * MAIN, 2 * A)
    rest = chain[:, MAIN:].reshape(N_Y * 8, 2 * A)
    full_ref[...] = jnp.concatenate([first, rest], axis=0).T
    half_rows(full_ref, far_ref, lax.axis_index("h"))


def last_kernel(after_ref, interp_ref, offsets_ref, last_ref):
    del after_ref
    mine = lax.axis_index("h")
    low = mine * (A - HALF)
    last = [
        band_t(interp_ref, offsets_ref, 4, mine, mine, low, HALF),
        band_t(interp_ref, offsets_ref, 4, mine, 1 - mine, low, HALF),
    ]
    last_ref[...] = jnp.concatenate(last, axis=0).T


def merge_kernel(after_ref, near_ref, own_ref, other_ref, out_ref):
    del after_ref
    size = N_Y * PER * REST
    order = one_hot(size, size, lambda r, c: c == r // 4 % 4 * (N_Y * REST) + r // 16 * 4 + r % 4)
    data = jnp.concatenate([own_ref[...], other_ref[...]], axis=0)
    made = jnp.dot(near_ref[...], data, preferred_element_type=F32)
    made = made.astype(BF16)
    for y in range(N_Y):
        for j in range(PER):
            out_ref[y, MAIN * j : MAIN * j + MAIN] = made[MAIN * y : MAIN * y + MAIN, 128 * j : 128 * j + 128]
    rest = made[N_Y * MAIN :]
    rest = jnp.concatenate([rest[:, 128 * j : 128 * j + 128] for j in range(PER)], axis=0)
    rest = jnp.dot(order, rest, preferred_element_type=F32).astype(BF16)
    for y in range(N_Y):
        out_ref[y, PER * MAIN :] = rest[16 * y : 16 * y + 16]


def join_kernel(far_ref, got_ref, send_ref, own_ref):
    order = one_hot(
        PER * N_Y * 8,
        N_Y * 16,
        lambda r, c: (c == r // 8 % N_Y * 16 + r // (8 * N_Y) * 4 + r % 8) & (r % 8 < REST),
    )
    rest = got_ref[:, PER * MAIN :, :].reshape(N_Y * 16, KTAP)
    rest = jnp.dot(order, rest, preferred_element_type=F32).astype(BF16)
    for j in range(PER):
        block = got_ref[:, MAIN * j : MAIN * j + MAIN, :].reshape(N_Y * MAIN, KTAP)
        block = jnp.concatenate([block, rest[8 * N_Y * j : 8 * N_Y * (j + 1)]], axis=0)
        made = jnp.dot(far_ref[...], block, preferred_element_type=F32).astype(BF16)
        send_ref[:, 128 * j : 128 * j + 128] = made[: 2 * HALF]
        own_ref[:, 128 * j : 128 * j + 128] = made[2 * HALF :]


def final_kernel(last_ref, own_ref, other_ref, out_ref):
    data = jnp.concatenate([own_ref[...], other_ref[...]], axis=0)
    made = jnp.dot(last_ref[...], data, preferred_element_type=F32).astype(BF16)
    out_ref[0] = made[:A]
    out_ref[1] = made[A:]


def call(body, ins, outs, scratch=(), limit=48):
    return pl.pallas_call(
        body,
        out_shape=[jax.ShapeDtypeStruct(shape, BF16) for shape in outs],
        in_specs=ins,
        out_specs=[VMEM] * len(outs),
        scratch_shapes=list(scratch),
        compiler_params=pltpu.CompilerParams(vmem_limit_bytes=limit * 2**20),
    )


def shards(raw, chirp, steer, offsets, interp, owner):
    x = raw.reshape(P_HERE, CH, 2, BLOCKS, KTAP).transpose(0, 1, 3, 2, 4)
    x = x.reshape(P_HERE, CH, 2 * BLOCKS, KTAP)
    packed, token = call(
        compress_kernel,
        [HBM] * 3,
        [(N_TILE, PER, 2, P_HERE, KTAP), (16, KTAP)],
        [
            pltpu.SMEM((N_TILE,), jnp.int32),
            pltpu.VMEM((CH, 2, KTAP), BF16),
            pltpu.VMEM((P_HERE, CH, 2 * BLOCKS, KTAP), BF16),
            pltpu.SMEM((N_TILE,), jnp.int32),
            pltpu.VMEM((4 * CH * KTAP, 2 * KTAP), BF16),
            pltpu.VMEM(((BLOCKS + 1) * P_HERE, 2 * CH * KTAP), BF16),
            pltpu.SemaphoreType.DMA((BLOCKS // 8 + 2,)),
        ],
        limit=60,
    )(owner, chirp, x)
    packed = packed.reshape(N_TILE, PER * 2 * P_HERE, KTAP)
    got = lax.all_to_all(packed, ("x", "l"), 0, 0, tiled=True)
    weights, near = call(
        prep_kernel,
        [VMEM] * 5,
        [(4 * HALF, 2 * P_G), (N_Y * (MAIN + REST), 4 * HALF)],
        [pltpu.VMEM((2 * A, 2 * P_G), F32)],
    )(token, steer, interp, offsets, jnp.asarray(row_pick()))
    send, own = call(project_kernel, [VMEM] * 2, [(2 * HALF, R)] * 2)(weights, got)
    other = lax.ppermute(send, "c", [(0, 1), (1, 0)])
    (far,) = call(
        far_kernel,
        [VMEM] * 3,
        [(4 * HALF, N_Y * FAR_ROWS)],
        [pltpu.VMEM((2 * A, N_Y * FAR_ROWS), F32)],
    )(own, interp, offsets)
    (pieces,) = call(merge_kernel, [VMEM] * 4, [(N_Y, PIECE, KTAP)])(far, near, own, other)
    parts = lax.all_to_all(pieces, "y", 0, 0, tiled=True)
    send, own = call(join_kernel, [VMEM] * 2, [(2 * HALF, R)] * 2)(far, parts)
    other = lax.ppermute(send, "h", [(0, 1), (1, 0)])
    (last,) = call(last_kernel, [VMEM] * 3, [(2 * A, 4 * HALF)])(own, interp, offsets)
    (image,) = call(final_kernel, [VMEM] * 3, [(2, A, R)])(last, own, other)
    return image


def solution(mesh):
    split = Mesh(mesh.devices.reshape(2, 8, 2, 4, 4), ("h", "y", "c", "x", "l"))
    pulse = ("h", "y", "c")
    tile = ("x", "l")
    placed = (P(pulse + tile, None, None, None), P(), P(pulse, None), P(), P(), P())
    return jax.shard_map(
        shards, mesh=split, in_specs=placed, out_specs=P(None, pulse, tile), check_vma=False
    )
```

```python
import math

import jax
import jax.numpy as jnp
import numpy as np
from jax import lax
from jax.experimental import pallas as pl
from jax.experimental.pallas import tpu as pltpu
from jax.sharding import Mesh
from jax.sharding import PartitionSpec as P

S = 8192
CH = 4
KTAP = 128
A = 128
KB = 4
R = 512
P_G = 256
N_TILE = 16
P_HERE = 16
BLOCKS = S // KTAP
PER = R // KTAP
WIN = 25
MAIN = 48
REST = 4
FAR_ROWS = 56
PIECE = PER * (MAIN + REST)
HALF = 72
N_Y = 8
F32 = jnp.float32
BF16 = jnp.bfloat16
VMEM = pl.BlockSpec(memory_space=pltpu.VMEM)
HBM = pl.BlockSpec(memory_space=pltpu.HBM)


def band_range(half, low, high):
    first = min(max((half * A + low) // 2 - KB // 2, 0), A - KB)
    last = min(max((half * A + high) // 2, 0), A - KB)
    return first, last + KB - 1


def window_lows():
    lows = []
    for y in range(N_Y):
        low, high = 0, A - 1
        for level in (3, 2, 1):
            low, high = band_range(y >> level - 1 & 1, low, high)
        assert high - low + 1 <= WIN
        lows.append(low)
    return lows


def row_pick():
    table = np.zeros((N_Y, MAIN + REST, 2, A), np.float32)
    for y, low in enumerate(window_lows()):
        for part in range(2):
            for i in range(min(WIN, A - low)):
                table[y, part * WIN + i, part, low + i] = 1
    table = table.reshape(N_Y, MAIN + REST, 2 * A)
    first = table[:, :MAIN].reshape(N_Y * MAIN, 2 * A)
    rest = table[:, MAIN:].reshape(N_Y * REST, 2 * A)
    return np.concatenate([first, rest]).astype(jnp.bfloat16)


def one_hot(rows, cols, wanted):
    row = lax.broadcasted_iota(jnp.int32, (rows, cols), 0)
    col = lax.broadcasted_iota(jnp.int32, (rows, cols), 1)
    return jnp.where(wanted(row, col), 1.0, 0.0).astype(BF16)


def compress_kernel(
    owner_hbm, chirp_hbm, x_hbm, out_ref, token_ref, owner_ref, chirp_ref, x_ref, inv_ref, table_ref, z_ref, sem
):
    steps = BLOCKS // 8
    loads = [
        pltpu.make_async_copy(
            x_hbm.at[:, :, 16 * g : 16 * g + 16, :], x_ref.at[:, :, 16 * g : 16 * g + 16, :], sem.at[g]
        )
        for g in range(steps)
    ]
    chirp_load = pltpu.make_async_copy(chirp_hbm, chirp_ref, sem.at[steps])
    owner_load = pltpu.make_async_copy(owner_hbm, owner_ref, sem.at[steps + 1])
    token_ref[...] = jnp.zeros(token_ref.shape, BF16)
    chirp_load.start()
    for load in loads:
        load.start()
    owner_load.start()
    row = lax.broadcasted_iota(jnp.int32, (KTAP, KTAP), 0)
    col = lax.broadcasted_iota(jnp.int32, (KTAP, KTAP), 1)
    flip = jnp.where((row + col) % KTAP == 0, 1.0, 0.0).astype(BF16)
    pick = one_hot(256, 256, lambda r, c: c == r % 16 * 16 + r // 16 % 8 * 2 + r // 128)
    half = CH * KTAP
    z_ref[BLOCKS * P_HERE :, :] = jnp.zeros((P_HERE, 2 * half), BF16)
    chirp_load.wait()
    for c in range(CH):
        taps = chirp_ref[c].astype(F32)
        for q in range(2):
            line = jnp.broadcast_to(taps[q : q + 1], (16, KTAP)).astype(BF16)
            line = jnp.dot(line, flip, preferred_element_type=F32)
            circ = jnp.broadcast_to(line[0:1], (KTAP, KTAP))
            circ = pltpu.roll(circ, 0, 1, stride=1, stride_axis=0)
            for upper in range(2):
                keep = (row < col) if upper else (row >= col)
                kept = jnp.where(keep, circ, 0.0)
                base = upper * 2 * half + c * KTAP
                if q == 0:
                    table_ref[base : base + KTAP, 0:KTAP] = kept.astype(BF16)
                    table_ref[base + half : base + half + KTAP, KTAP:] = kept.astype(BF16)
                else:
                    table_ref[base : base + KTAP, KTAP:] = kept.astype(BF16)
                    table_ref[base + half : base + half + KTAP, 0:KTAP] = (-kept).astype(BF16)
    owner_load.wait()
    for t in range(N_TILE):
        inv_ref[owner_ref[t]] = t
    def convolve(m):
        lower = z_ref[256 * m : 256 * m + 256, :]
        upper = z_ref[256 * m + 16 : 256 * m + 272, :]
        acc = jnp.dot(lower, table_ref[0 : 2 * half, :], preferred_element_type=F32)
        acc = acc + jnp.dot(upper, table_ref[2 * half :, :], preferred_element_type=F32)
        acc = acc.astype(BF16)
        for n in range(4):
            to = inv_ref[4 * m + n]
            for j in range(PER):
                base = 16 * (PER * n + j)
                for o in range(2):
                    out_ref[to, j, o] = acc[base : base + 16, 128 * o : 128 * o + 128]


    def gather(g):
        parts = []
        for c in range(CH):
            got = x_ref[:, c, 16 * g : 16 * g + 16, :]
            parts.append(got.reshape(256, KTAP))
        moved = jnp.dot(pick, jnp.concatenate(parts, axis=1), preferred_element_type=F32)
        moved = moved.astype(BF16)
        z_ref[128 * g : 128 * g + 128, 0:half] = moved[0:128]
        z_ref[128 * g : 128 * g + 128, half:] = moved[128:256]

    for load in loads[0:4]:
        load.wait()
    for g in range(0, 4):
        gather(g)
    for load in loads[4:8]:
        load.wait()
    for g in range(4, 8):
        gather(g)
    convolve(0)
    convolve(1)
    convolve(2)
    convolve(3)


def band_parts(interp_ref, offsets_ref, level, half, child, rows):
    both = offsets_ref[level]
    starts = jnp.where(half == 0, both[0:1], both[1:2])
    delta = rows - starts
    real = jnp.zeros(rows.shape, F32)
    imag = jnp.zeros(rows.shape, F32)
    for k in range(KB):
        taps = interp_ref[level, half, child, k].astype(F32)
        hit = delta == k
        real = jnp.where(hit, taps[0:1], real)
        imag = jnp.where(hit, taps[1:2], imag)
    return real, imag


def band_t(interp_ref, offsets_ref, level, half, child, low, count):
    rows = lax.broadcasted_iota(jnp.int32, (count, A), 0) + low
    real, imag = band_parts(interp_ref, offsets_ref, level, half, child, rows)
    upper = jnp.concatenate([real, imag], axis=1)
    lower = jnp.concatenate([-imag, real], axis=1)
    return jnp.concatenate([upper, lower], axis=0).astype(BF16)


def prep_kernel(after_ref, steer_ref, interp_ref, offsets_ref, pick_ref, weights_ref, near_ref, w_ref):
    del after_ref
    mine = lax.axis_index("c")
    theta = steer_ref[...]
    scale = 1.0 / math.sqrt(P_G)
    cos_part = (jnp.cos(theta) * scale).astype(BF16).reshape(N_TILE, P_HERE, A)
    sin_part = (jnp.sin(theta) * scale).astype(BF16).reshape(N_TILE, P_HERE, A)
    first = jnp.concatenate([cos_part, sin_part], axis=2)
    second = jnp.concatenate([-sin_part, cos_part], axis=2)
    full = jnp.stack([first, second], axis=1).reshape(2 * P_G, 2 * A)
    w_ref[...] = full.T.astype(F32)
    half_rows(w_ref, weights_ref, mine)
    low = mine * (A - HALF)
    near = [
        band_t(interp_ref, offsets_ref, 0, mine, mine, low, HALF),
        band_t(interp_ref, offsets_ref, 0, mine, 1 - mine, low, HALF),
    ]
    near = jnp.concatenate(near, axis=0)
    nt = (((1,), (1,)), ((), ()))
    near_ref[...] = lax.dot_general(pick_ref[...], near, nt, preferred_element_type=F32).astype(BF16)


def half_rows(full_ref, out_ref, mine):
    for n, side in enumerate((1 - mine, mine)):
        for part in range(2):
            low = pl.multiple_of(part * A + side * (A - HALF), 8)
            at = (2 * n + part) * HALF
            out_ref[at : at + HALF, :] = full_ref[pl.ds(low, HALF), :].astype(BF16)


def project_kernel(weights_ref, got_ref, send_ref, own_ref):
    for j in range(PER):
        block = got_ref[:, 32 * j : 32 * j + 32, :].reshape(2 * P_G, KTAP)
        made = jnp.dot(weights_ref[...], block, preferred_element_type=F32).astype(BF16)
        send_ref[:, 128 * j : 128 * j + 128] = made[: 2 * HALF]
        own_ref[:, 128 * j : 128 * j + 128] = made[2 * HALF :]


def far_kernel(after_ref, interp_ref, offsets_ref, far_ref, full_ref):
    del after_ref
    y = lax.axis_index("y")
    bits = [y & 1, y >> 1 & 1, y >> 2 & 1]
    low = jnp.int32(0)
    for bit in reversed(bits):
        low = jnp.clip((bit * A + low) // 2 - KB // 2, 0, A - KB)
    n = lax.broadcasted_iota(jnp.int32, (FAR_ROWS, A), 0)
    second = n >= WIN
    rows = low + n - jnp.where(second, WIN, 0)
    chain = []
    for q in range(2):
        real, imag = band_parts(interp_ref, offsets_ref, 1, bits[0], q, rows)
        left = jnp.where(second, -imag, real)
        right = jnp.where(second, real, imag)
        chain.append(jnp.concatenate([left, right], axis=1))
    chain = jnp.concatenate(chain, axis=0)
    for level in range(2, 4):
        grown = []
        for q in range(2):
            step = band_t(interp_ref, offsets_ref, level, bits[level - 1], q, 0, A)
            grown.append(jnp.dot(chain.astype(BF16), step, preferred_element_type=F32))
        chain = jnp.concatenate(grown, axis=0)
    chain = chain.reshape(N_Y, FAR_ROWS, 2 * A)
    first = chain[:, :MAIN].reshape(N_Y * MAIN, 2 * A)
    rest = chain[:, MAIN:].reshape(N_Y * 8, 2 * A)
    full_ref[...] = jnp.concatenate([first, rest], axis=0).T
    half_rows(full_ref, far_ref, lax.axis_index("h"))


def last_kernel(after_ref, interp_ref, offsets_ref, last_ref):
    del after_ref
    mine = lax.axis_index("h")
    low = mine * (A - HALF)
    last = [
        band_t(interp_ref, offsets_ref, 4, mine, mine, low, HALF),
        band_t(interp_ref, offsets_ref, 4, mine, 1 - mine, low, HALF),
    ]
    last_ref[...] = jnp.concatenate(last, axis=0).T


def merge_kernel(after_ref, near_ref, own_ref, other_ref, out_ref):
    del after_ref
    size = N_Y * PER * REST
    order = one_hot(size, size, lambda r, c: c == r // 4 % 4 * (N_Y * REST) + r // 16 * 4 + r % 4)
    data = jnp.concatenate([own_ref[...], other_ref[...]], axis=0)
    made = jnp.dot(near_ref[...], data, preferred_element_type=F32)
    made = made.astype(BF16)
    for y in range(N_Y):
        for j in range(PER):
            out_ref[y, MAIN * j : MAIN * j + MAIN] = made[MAIN * y : MAIN * y + MAIN, 128 * j : 128 * j + 128]
    rest = made[N_Y * MAIN :]
    rest = jnp.concatenate([rest[:, 128 * j : 128 * j + 128] for j in range(PER)], axis=0)
    rest = jnp.dot(order, rest, preferred_element_type=F32).astype(BF16)
    for y in range(N_Y):
        out_ref[y, PER * MAIN :] = rest[16 * y : 16 * y + 16]


def join_kernel(far_ref, got_ref, send_ref, own_ref):
    order = one_hot(
        PER * N_Y * 8,
        N_Y * 16,
        lambda r, c: (c == r // 8 % N_Y * 16 + r // (8 * N_Y) * 4 + r % 8) & (r % 8 < REST),
    )
    rest = got_ref[:, PER * MAIN :, :].reshape(N_Y * 16, KTAP)
    rest = jnp.dot(order, rest, preferred_element_type=F32).astype(BF16)
    for j in range(PER):
        block = got_ref[:, MAIN * j : MAIN * j + MAIN, :].reshape(N_Y * MAIN, KTAP)
        block = jnp.concatenate([block, rest[8 * N_Y * j : 8 * N_Y * (j + 1)]], axis=0)
        made = jnp.dot(far_ref[...], block, preferred_element_type=F32).astype(BF16)
        send_ref[:, 128 * j : 128 * j + 128] = made[: 2 * HALF]
        own_ref[:, 128 * j : 128 * j + 128] = made[2 * HALF :]


def final_kernel(last_ref, own_ref, other_ref, out_ref):
    data = jnp.concatenate([own_ref[...], other_ref[...]], axis=0)
    made = jnp.dot(last_ref[...], data, preferred_element_type=F32).astype(BF16)
    out_ref[0] = made[:A]
    out_ref[1] = made[A:]


def call(body, ins, outs, scratch=(), limit=48):
    return pl.pallas_call(
        body,
        out_shape=[jax.ShapeDtypeStruct(shape, BF16) for shape in outs],
        in_specs=ins,
        out_specs=[VMEM] * len(outs),
        scratch_shapes=list(scratch),
        compiler_params=pltpu.CompilerParams(vmem_limit_bytes=limit * 2**20),
    )


def run_compress(owner, chirp, x):
    return call(
        compress_kernel,
        [HBM] * 3,
        [(N_TILE, PER, 2, P_HERE, KTAP), (16, KTAP)],
        [
            pltpu.SMEM((N_TILE,), jnp.int32),
            pltpu.VMEM((CH, 2, KTAP), BF16),
            pltpu.VMEM((P_HERE, CH, 2 * BLOCKS, KTAP), BF16),
            pltpu.SMEM((N_TILE,), jnp.int32),
            pltpu.VMEM((4 * CH * KTAP, 2 * KTAP), BF16),
            pltpu.VMEM(((BLOCKS + 1) * P_HERE, 2 * CH * KTAP), BF16),
            pltpu.SemaphoreType.DMA((BLOCKS // 8 + 2,)),
        ],
        limit=60,
    )(owner, chirp, x)


def shards(raw, chirp, steer, offsets, interp, owner):
    x = raw.reshape(P_HERE, CH, 2, BLOCKS, KTAP).transpose(0, 1, 3, 2, 4)
    x = x.reshape(P_HERE, CH, 2 * BLOCKS, KTAP)
    packed, token = run_compress(owner, chirp, x)
    packed = packed.reshape(N_TILE, PER * 2 * P_HERE, KTAP)
    got = lax.all_to_all(packed, ("x", "l"), 0, 0, tiled=True)
    weights, near = call(
        prep_kernel,
        [VMEM] * 5,
        [(4 * HALF, 2 * P_G), (N_Y * (MAIN + REST), 4 * HALF)],
        [pltpu.VMEM((2 * A, 2 * P_G), F32)],
    )(token, steer, interp, offsets, jnp.asarray(row_pick()))
    send, own = call(project_kernel, [VMEM] * 2, [(2 * HALF, R)] * 2)(weights, got)
    other = lax.ppermute(send, "c", [(0, 1), (1, 0)])
    (far,) = call(
        far_kernel,
        [VMEM] * 3,
        [(4 * HALF, N_Y * FAR_ROWS)],
        [pltpu.VMEM((2 * A, N_Y * FAR_ROWS), F32)],
    )(own, interp, offsets)
    (pieces,) = call(merge_kernel, [VMEM] * 4, [(N_Y, PIECE, KTAP)])(far, near, own, other)
    parts = lax.all_to_all(pieces, "y", 0, 0, tiled=True)
    send, own = call(join_kernel, [VMEM] * 2, [(2 * HALF, R)] * 2)(far, parts)
    other = lax.ppermute(send, "h", [(0, 1), (1, 0)])
    (last,) = call(last_kernel, [VMEM] * 3, [(2 * A, 4 * HALF)])(own, interp, offsets)
    (image,) = call(final_kernel, [VMEM] * 3, [(2, A, R)])(last, own, other)
    return image


def solution(mesh):
    split = Mesh(mesh.devices.reshape(2, 8, 2, 4, 4), ("h", "y", "c", "x", "l"))
    pulse = ("h", "y", "c")
    tile = ("x", "l")
    placed = (P(pulse + tile, None, None, None), P(), P(pulse, None), P(), P(), P())
    return jax.shard_map(
        shards, mesh=split, in_specs=placed, out_specs=P(None, pulse, tile), check_vma=False
    )
```

```python
import math

import jax
import jax.numpy as jnp
import numpy as np
from jax import lax
from jax.experimental import pallas as pl
from jax.experimental.pallas import tpu as pltpu
from jax.sharding import Mesh
from jax.sharding import PartitionSpec as P

S = 8192
CH = 4
KTAP = 128
A = 128
KB = 4
R = 512
P_G = 256
N_TILE = 16
P_HERE = 16
BLOCKS = S // KTAP
PER = R // KTAP
WIN = 25
MAIN = 48
REST = 4
FAR_ROWS = 56
PIECE = PER * (MAIN + REST)
HALF = 72
N_Y = 8
F32 = jnp.float32
BF16 = jnp.bfloat16
VMEM = pl.BlockSpec(memory_space=pltpu.VMEM)
HBM = pl.BlockSpec(memory_space=pltpu.HBM)


def band_range(half, low, high):
    first = min(max((half * A + low) // 2 - KB // 2, 0), A - KB)
    last = min(max((half * A + high) // 2, 0), A - KB)
    return first, last + KB - 1


def window_lows():
    lows = []
    for y in range(N_Y):
        low, high = 0, A - 1
        for level in (3, 2, 1):
            low, high = band_range(y >> level - 1 & 1, low, high)
        assert high - low + 1 <= WIN
        lows.append(low)
    return lows


def row_pick():
    table = np.zeros((N_Y, MAIN + REST, 2, A), np.float32)
    for y, low in enumerate(window_lows()):
        for part in range(2):
            for i in range(min(WIN, A - low)):
                table[y, part * WIN + i, part, low + i] = 1
    table = table.reshape(N_Y, MAIN + REST, 2 * A)
    first = table[:, :MAIN].reshape(N_Y * MAIN, 2 * A)
    rest = table[:, MAIN:].reshape(N_Y * REST, 2 * A)
    return np.concatenate([first, rest]).astype(jnp.bfloat16)


def one_hot(rows, cols, wanted):
    row = lax.broadcasted_iota(jnp.int32, (rows, cols), 0)
    col = lax.broadcasted_iota(jnp.int32, (rows, cols), 1)
    return jnp.where(wanted(row, col), 1.0, 0.0).astype(BF16)


def compress_kernel(
    owner_hbm, chirp_hbm, x_hbm, out_ref, token_ref, owner_ref, chirp_ref, x_ref, inv_ref, table_ref, z_ref, sem
):
    steps = BLOCKS // 8
    loads = [
        pltpu.make_async_copy(
            x_hbm.at[:, :, 16 * g : 16 * g + 16, :], x_ref.at[:, :, 16 * g : 16 * g + 16, :], sem.at[g]
        )
        for g in range(steps)
    ]
    chirp_load = pltpu.make_async_copy(chirp_hbm, chirp_ref, sem.at[steps])
    owner_load = pltpu.make_async_copy(owner_hbm, owner_ref, sem.at[steps + 1])
    token_ref[...] = jnp.zeros(token_ref.shape, BF16)
    chirp_load.start()
    for load in loads:
        load.start()
    owner_load.start()
    row = lax.broadcasted_iota(jnp.int32, (KTAP, KTAP), 0)
    col = lax.broadcasted_iota(jnp.int32, (KTAP, KTAP), 1)
    flip = jnp.where((row + col) % KTAP == 0, 1.0, 0.0).astype(BF16)
    pick = one_hot(256, 256, lambda r, c: c == r % 16 * 16 + r // 16 % 8 * 2 + r // 128)
    half = CH * KTAP
    z_ref[BLOCKS * P_HERE :, :] = jnp.zeros((P_HERE, 2 * half), BF16)
    chirp_load.wait()
    for c in range(CH):
        taps = chirp_ref[c].astype(F32)
        for q in range(2):
            line = jnp.broadcast_to(taps[q : q + 1], (16, KTAP)).astype(BF16)
            line = jnp.dot(line, flip, preferred_element_type=F32)
            circ = jnp.broadcast_to(line[0:1], (KTAP, KTAP))
            circ = pltpu.roll(circ, 0, 1, stride=1, stride_axis=0)
            for upper in range(2):
                keep = (row < col) if upper else (row >= col)
                kept = jnp.where(keep, circ, 0.0)
                base = upper * 2 * half + c * KTAP
                if q == 0:
                    table_ref[base : base + KTAP, 0:KTAP] = kept.astype(BF16)
                    table_ref[base + half : base + half + KTAP, KTAP:] = kept.astype(BF16)
                else:
                    table_ref[base : base + KTAP, KTAP:] = kept.astype(BF16)
                    table_ref[base + half : base + half + KTAP, 0:KTAP] = (-kept).astype(BF16)
    owner_load.wait()
    for t in range(N_TILE):
        inv_ref[owner_ref[t]] = t
    def convolve(m):
        lower = z_ref[256 * m : 256 * m + 256, :]
        upper = z_ref[256 * m + 16 : 256 * m + 272, :]
        acc = jnp.dot(lower, table_ref[0 : 2 * half, :], preferred_element_type=F32)
        acc = acc + jnp.dot(upper, table_ref[2 * half :, :], preferred_element_type=F32)
        acc = acc.astype(BF16)
        for n in range(4):
            to = inv_ref[4 * m + n]
            for j in range(PER):
                base = 16 * (PER * n + j)
                for o in range(2):
                    out_ref[to, j, o] = acc[base : base + 16, 128 * o : 128 * o + 128]


    def gather(g):
        parts = []
        for c in range(CH):
            got = x_ref[:, c, 16 * g : 16 * g + 16, :]
            parts.append(got.reshape(256, KTAP))
        moved = jnp.dot(pick, jnp.concatenate(parts, axis=1), preferred_element_type=F32)
        moved = moved.astype(BF16)
        z_ref[128 * g : 128 * g + 128, 0:half] = moved[0:128]
        z_ref[128 * g : 128 * g + 128, half:] = moved[128:256]

    for load in loads[0:4]:
        load.wait()
    for g in range(0, 4):
        gather(g)
    for load in loads[4:8]:
        load.wait()
    for g in range(4, 8):
        gather(g)
    convolve(0)
    convolve(1)
    convolve(2)
    convolve(3)


def band_parts(interp_ref, offsets_ref, level, half, child, rows):
    both = offsets_ref[level]
    starts = jnp.where(half == 0, both[0:1], both[1:2])
    delta = rows - starts
    real = jnp.zeros(rows.shape, F32)
    imag = jnp.zeros(rows.shape, F32)
    for k in range(KB):
        taps = interp_ref[level, half, child, k].astype(F32)
        hit = delta == k
        real = jnp.where(hit, taps[0:1], real)
        imag = jnp.where(hit, taps[1:2], imag)
    return real, imag


def band_t(interp_ref, offsets_ref, level, half, child, low, count):
    rows = lax.broadcasted_iota(jnp.int32, (count, A), 0) + low
    real, imag = band_parts(interp_ref, offsets_ref, level, half, child, rows)
    upper = jnp.concatenate([real, imag], axis=1)
    lower = jnp.concatenate([-imag, real], axis=1)
    return jnp.concatenate([upper, lower], axis=0).astype(BF16)


def prep_kernel(after_ref, steer_ref, interp_ref, offsets_ref, pick_ref, weights_ref, near_ref, w_ref):
    del after_ref
    mine = lax.axis_index("c")
    theta = steer_ref[...]
    scale = 1.0 / math.sqrt(P_G)
    cos_part = (jnp.cos(theta) * scale).astype(BF16).reshape(N_TILE, P_HERE, A)
    sin_part = (jnp.sin(theta) * scale).astype(BF16).reshape(N_TILE, P_HERE, A)
    first = jnp.concatenate([cos_part, sin_part], axis=2)
    second = jnp.concatenate([-sin_part, cos_part], axis=2)
    full = jnp.stack([first, second], axis=1).reshape(2 * P_G, 2 * A)
    w_ref[...] = full.T.astype(F32)
    half_rows(w_ref, weights_ref, mine)
    low = mine * (A - HALF)
    near = [
        band_t(interp_ref, offsets_ref, 0, mine, mine, low, HALF),
        band_t(interp_ref, offsets_ref, 0, mine, 1 - mine, low, HALF),
    ]
    near = jnp.concatenate(near, axis=0)
    nt = (((1,), (1,)), ((), ()))
    near_ref[...] = lax.dot_general(pick_ref[...], near, nt, preferred_element_type=F32).astype(BF16)


def half_rows(full_ref, out_ref, mine):
    rows = []
    for side in (1 - mine, mine):
        for part in range(2):
            low = pl.multiple_of(part * A + side * (A - HALF), 8)
            rows.append(full_ref[pl.ds(low, HALF), :])
    out_ref[...] = jnp.concatenate(rows, axis=0).astype(BF16)


def project_kernel(weights_ref, got_ref, send_ref, own_ref):
    for j in range(PER):
        block = got_ref[:, 32 * j : 32 * j + 32, :].reshape(2 * P_G, KTAP)
        made = jnp.dot(weights_ref[...], block, preferred_element_type=F32).astype(BF16)
        send_ref[:, 128 * j : 128 * j + 128] = made[: 2 * HALF]
        own_ref[:, 128 * j : 128 * j + 128] = made[2 * HALF :]


def far_kernel(after_ref, interp_ref, offsets_ref, far_ref, full_ref):
    del after_ref
    y = lax.axis_index("y")
    bits = [y & 1, y >> 1 & 1, y >> 2 & 1]
    low = jnp.int32(0)
    for bit in reversed(bits):
        low = jnp.clip((bit * A + low) // 2 - KB // 2, 0, A - KB)
    n = lax.broadcasted_iota(jnp.int32, (FAR_ROWS, A), 0)
    second = n >= WIN
    rows = low + n - jnp.where(second, WIN, 0)
    chain = []
    for q in range(2):
        real, imag = band_parts(interp_ref, offsets_ref, 1, bits[0], q, rows)
        left = jnp.where(second, -imag, real)
        right = jnp.where(second, real, imag)
        chain.append(jnp.concatenate([left, right], axis=1))
    chain = jnp.concatenate(chain, axis=0)
    for level in range(2, 4):
        grown = []
        for q in range(2):
            step = band_t(interp_ref, offsets_ref, level, bits[level - 1], q, 0, A)
            grown.append(jnp.dot(chain.astype(BF16), step, preferred_element_type=F32))
        chain = jnp.concatenate(grown, axis=0)
    chain = chain.reshape(N_Y, FAR_ROWS, 2 * A)
    first = chain[:, :MAIN].reshape(N_Y * MAIN, 2 * A)
    rest = chain[:, MAIN:].reshape(N_Y * 8, 2 * A)
    full_ref[...] = jnp.concatenate([first, rest], axis=0).T
    half_rows(full_ref, far_ref, lax.axis_index("h"))


def last_kernel(after_ref, interp_ref, offsets_ref, last_ref):
    del after_ref
    mine = lax.axis_index("h")
    low = mine * (A - HALF)
    last = [
        band_t(interp_ref, offsets_ref, 4, mine, mine, low, HALF),
        band_t(interp_ref, offsets_ref, 4, mine, 1 - mine, low, HALF),
    ]
    last_ref[...] = jnp.concatenate(last, axis=0).T


def merge_kernel(after_ref, near_ref, own_ref, other_ref, out_ref):
    del after_ref
    size = N_Y * PER * REST
    order = one_hot(size, size, lambda r, c: c == r // 4 % 4 * (N_Y * REST) + r // 16 * 4 + r % 4)
    data = jnp.concatenate([own_ref[...], other_ref[...]], axis=0)
    made = jnp.dot(near_ref[...], data, preferred_element_type=F32)
    made = made.astype(BF16)
    for y in range(N_Y):
        for j in range(PER):
            out_ref[y, MAIN * j : MAIN * j + MAIN] = made[MAIN * y : MAIN * y + MAIN, 128 * j : 128 * j + 128]
    rest = made[N_Y * MAIN :]
    rest = jnp.concatenate([rest[:, 128 * j : 128 * j + 128] for j in range(PER)], axis=0)
    rest = jnp.dot(order, rest, preferred_element_type=F32).astype(BF16)
    for y in range(N_Y):
        out_ref[y, PER * MAIN :] = rest[16 * y : 16 * y + 16]


def join_kernel(far_ref, got_ref, send_ref, own_ref):
    order = one_hot(
        PER * N_Y * 8,
        N_Y * 16,
        lambda r, c: (c == r // 8 % N_Y * 16 + r // (8 * N_Y) * 4 + r % 8) & (r % 8 < REST),
    )
    rest = got_ref[:, PER * MAIN :, :].reshape(N_Y * 16, KTAP)
    rest = jnp.dot(order, rest, preferred_element_type=F32).astype(BF16)
    for j in range(PER):
        block = got_ref[:, MAIN * j : MAIN * j + MAIN, :].reshape(N_Y * MAIN, KTAP)
        block = jnp.concatenate([block, rest[8 * N_Y * j : 8 * N_Y * (j + 1)]], axis=0)
        made = jnp.dot(far_ref[...], block, preferred_element_type=F32).astype(BF16)
        send_ref[:, 128 * j : 128 * j + 128] = made[: 2 * HALF]
        own_ref[:, 128 * j : 128 * j + 128] = made[2 * HALF :]


def final_kernel(last_ref, own_ref, other_ref, out_ref):
    data = jnp.concatenate([own_ref[...], other_ref[...]], axis=0)
    made = jnp.dot(last_ref[...], data, preferred_element_type=F32).astype(BF16)
    out_ref[0] = made[:A]
    out_ref[1] = made[A:]


def call(body, ins, outs, scratch=(), limit=48):
    return pl.pallas_call(
        body,
        out_shape=[jax.ShapeDtypeStruct(shape, BF16) for shape in outs],
        in_specs=ins,
        out_specs=[VMEM] * len(outs),
        scratch_shapes=list(scratch),
        compiler_params=pltpu.CompilerParams(vmem_limit_bytes=limit * 2**20),
    )


def run_compress(owner, chirp, x):
    return call(
        compress_kernel,
        [HBM] * 3,
        [(N_TILE, PER, 2, P_HERE, KTAP), (16, KTAP)],
        [
            pltpu.SMEM((N_TILE,), jnp.int32),
            pltpu.VMEM((CH, 2, KTAP), BF16),
            pltpu.VMEM((P_HERE, CH, 2 * BLOCKS, KTAP), BF16),
            pltpu.SMEM((N_TILE,), jnp.int32),
            pltpu.VMEM((4 * CH * KTAP, 2 * KTAP), BF16),
            pltpu.VMEM(((BLOCKS + 1) * P_HERE, 2 * CH * KTAP), BF16),
            pltpu.SemaphoreType.DMA((BLOCKS // 8 + 2,)),
        ],
        limit=60,
    )(owner, chirp, x)


def shards(raw, chirp, steer, offsets, interp, owner):
    x = raw.reshape(P_HERE, CH, 2, BLOCKS, KTAP).transpose(0, 1, 3, 2, 4)
    x = x.reshape(P_HERE, CH, 2 * BLOCKS, KTAP)
    packed, token = run_compress(owner, chirp, x)
    packed = packed.reshape(N_TILE, PER * 2 * P_HERE, KTAP)
    got = lax.all_to_all(packed, ("x", "l"), 0, 0, tiled=True)
    weights, near = call(
        prep_kernel,
        [VMEM] * 5,
        [(4 * HALF, 2 * P_G), (N_Y * (MAIN + REST), 4 * HALF)],
        [pltpu.VMEM((2 * A, 2 * P_G), F32)],
    )(token, steer, interp, offsets, jnp.asarray(row_pick()))
    send, own = call(project_kernel, [VMEM] * 2, [(2 * HALF, R)] * 2)(weights, got)
    other = lax.ppermute(send, "c", [(0, 1), (1, 0)])
    (far,) = call(
        far_kernel,
        [VMEM] * 3,
        [(4 * HALF, N_Y * FAR_ROWS)],
        [pltpu.VMEM((2 * A, N_Y * FAR_ROWS), F32)],
    )(own, interp, offsets)
    (pieces,) = call(merge_kernel, [VMEM] * 4, [(N_Y, PIECE, KTAP)])(far, near, own, other)
    parts = lax.all_to_all(pieces, "y", 0, 0, tiled=True)
    send, own = call(join_kernel, [VMEM] * 2, [(2 * HALF, R)] * 2)(far, parts)
    other = lax.ppermute(send, "h", [(0, 1), (1, 0)])
    (last,) = call(last_kernel, [VMEM] * 3, [(2 * A, 4 * HALF)])(own, interp, offsets)
    (image,) = call(final_kernel, [VMEM] * 3, [(2, A, R)])(last, own, other)
    return image


def solution(mesh):
    split = Mesh(mesh.devices.reshape(2, 8, 2, 4, 4), ("h", "y", "c", "x", "l"))
    pulse = ("h", "y", "c")
    tile = ("x", "l")
    placed = (P(pulse + tile, None, None, None), P(), P(pulse, None), P(), P(), P())
    return jax.shard_map(
        shards, mesh=split, in_specs=placed, out_specs=P(None, pulse, tile), check_vma=False
    )
```

```python
import functools
import math

import jax
import jax.numpy as jnp
import numpy as np
from jax import lax
from jax.experimental import pallas as pl
from jax.experimental.pallas import tpu as pltpu
from jax.sharding import Mesh
from jax.sharding import PartitionSpec as P

S = 8192
CH = 4
KTAP = 128
A = 128
KB = 4
R = 512
P_G = 256
N_TILE = 16
P_HERE = 16
BLOCKS = S // KTAP
PER = R // KTAP
WIN = 25
MAIN = 48
REST = 4
FAR_ROWS = 56
PIECE = PER * (MAIN + REST)
HALF = 72
N_Y = 8
F32 = jnp.float32
BF16 = jnp.bfloat16
VMEM = pl.BlockSpec(memory_space=pltpu.VMEM)
HBM = pl.BlockSpec(memory_space=pltpu.HBM)


def band_range(half, low, high):
    first = min(max((half * A + low) // 2 - KB // 2, 0), A - KB)
    last = min(max((half * A + high) // 2, 0), A - KB)
    return first, last + KB - 1


def window_lows():
    lows = []
    for y in range(N_Y):
        low, high = 0, A - 1
        for level in (3, 2, 1):
            low, high = band_range(y >> level - 1 & 1, low, high)
        assert high - low + 1 <= WIN
        lows.append(low)
    return lows


def row_pick():
    table = np.zeros((N_Y, MAIN + REST, 2, A), np.float32)
    for y, low in enumerate(window_lows()):
        for part in range(2):
            for i in range(min(WIN, A - low)):
                table[y, part * WIN + i, part, low + i] = 1
    table = table.reshape(N_Y, MAIN + REST, 2 * A)
    first = table[:, :MAIN].reshape(N_Y * MAIN, 2 * A)
    rest = table[:, MAIN:].reshape(N_Y * REST, 2 * A)
    return np.concatenate([first, rest]).astype(jnp.bfloat16)


def one_hot(rows, cols, wanted):
    row = lax.broadcasted_iota(jnp.int32, (rows, cols), 0)
    col = lax.broadcasted_iota(jnp.int32, (rows, cols), 1)
    return jnp.where(wanted(row, col), 1.0, 0.0).astype(BF16)


def compress_kernel(
    owner_hbm, chirp_hbm, x_hbm, out_ref, token_ref, owner_ref, chirp_ref, x_ref, inv_ref, table_ref, z_ref, sem
):
    steps = BLOCKS // 8
    loads = [
        pltpu.make_async_copy(
            x_hbm.at[:, :, 16 * g : 16 * g + 16, :], x_ref.at[:, :, 16 * g : 16 * g + 16, :], sem.at[g]
        )
        for g in range(steps)
    ]
    chirp_load = pltpu.make_async_copy(chirp_hbm, chirp_ref, sem.at[steps])
    owner_load = pltpu.make_async_copy(owner_hbm, owner_ref, sem.at[steps + 1])
    token_ref[...] = jnp.zeros(token_ref.shape, BF16)
    chirp_load.start()
    for load in loads:
        load.start()
    owner_load.start()
    row = lax.broadcasted_iota(jnp.int32, (KTAP, KTAP), 0)
    col = lax.broadcasted_iota(jnp.int32, (KTAP, KTAP), 1)
    flip = jnp.where((row + col) % KTAP == 0, 1.0, 0.0).astype(BF16)
    pick = one_hot(256, 256, lambda r, c: c == r % 16 * 16 + r // 16 % 8 * 2 + r // 128)
    half = CH * KTAP
    z_ref[BLOCKS * P_HERE :, :] = jnp.zeros((P_HERE, 2 * half), BF16)
    chirp_load.wait()
    for c in range(CH):
        taps = chirp_ref[c].astype(F32)
        for q in range(2):
            line = jnp.broadcast_to(taps[q : q + 1], (16, KTAP)).astype(BF16)
            line = jnp.dot(line, flip, preferred_element_type=F32)
            circ = jnp.broadcast_to(line[0:1], (KTAP, KTAP))
            circ = pltpu.roll(circ, 0, 1, stride=1, stride_axis=0)
            for upper in range(2):
                keep = (row < col) if upper else (row >= col)
                kept = jnp.where(keep, circ, 0.0)
                base = upper * 2 * half + c * KTAP
                if q == 0:
                    table_ref[base : base + KTAP, 0:KTAP] = kept.astype(BF16)
                    table_ref[base + half : base + half + KTAP, KTAP:] = kept.astype(BF16)
                else:
                    table_ref[base : base + KTAP, KTAP:] = kept.astype(BF16)
                    table_ref[base + half : base + half + KTAP, 0:KTAP] = (-kept).astype(BF16)
    owner_load.wait()
    for t in range(N_TILE):
        inv_ref[owner_ref[t]] = t
    def convolve(m):
        lower = z_ref[256 * m : 256 * m + 256, :]
        upper = z_ref[256 * m + 16 : 256 * m + 272, :]
        acc = jnp.dot(lower, table_ref[0 : 2 * half, :], preferred_element_type=F32)
        acc = acc + jnp.dot(upper, table_ref[2 * half :, :], preferred_element_type=F32)
        acc = acc.astype(BF16)
        for n in range(4):
            to = inv_ref[4 * m + n]
            for j in range(PER):
                base = 16 * (PER * n + j)
                for o in range(2):
                    out_ref[to, j, o] = acc[base : base + 16, 128 * o : 128 * o + 128]


    def gather(g):
        parts = []
        for c in range(CH):
            got = x_ref[:, c, 16 * g : 16 * g + 16, :]
            parts.append(got.reshape(256, KTAP))
        moved = jnp.dot(pick, jnp.concatenate(parts, axis=1), preferred_element_type=F32)
        moved = moved.astype(BF16)
        z_ref[128 * g : 128 * g + 128, 0:half] = moved[0:128]
        z_ref[128 * g : 128 * g + 128, half:] = moved[128:256]

    for load in loads[0:4]:
        load.wait()
    for g in range(0, 4):
        gather(g)
    for load in loads[4:8]:
        load.wait()
    for g in range(4, 8):
        gather(g)
    convolve(0)
    convolve(1)
    convolve(2)
    convolve(3)


def band_parts(interp_ref, offsets_ref, level, half, child, rows):
    both = offsets_ref[level]
    starts = jnp.where(half == 0, both[0:1], both[1:2])
    delta = rows - starts
    real = jnp.zeros(rows.shape, F32)
    imag = jnp.zeros(rows.shape, F32)
    for k in range(KB):
        taps = interp_ref[level, half, child, k].astype(F32)
        hit = delta == k
        real = jnp.where(hit, taps[0:1], real)
        imag = jnp.where(hit, taps[1:2], imag)
    return real, imag


def band_t(interp_ref, offsets_ref, level, half, child, low, count):
    rows = lax.broadcasted_iota(jnp.int32, (count, A), 0) + low
    real, imag = band_parts(interp_ref, offsets_ref, level, half, child, rows)
    upper = jnp.concatenate([real, imag], axis=1)
    lower = jnp.concatenate([-imag, real], axis=1)
    return jnp.concatenate([upper, lower], axis=0).astype(BF16)


def prep_kernel(after_ref, steer_ref, interp_ref, offsets_ref, pick_ref, weights_ref, near_ref, w_ref):
    del after_ref
    mine = lax.axis_index("c")
    theta = steer_ref[...]
    scale = 1.0 / math.sqrt(P_G)
    cos_part = (jnp.cos(theta) * scale).astype(BF16).reshape(N_TILE, P_HERE, A)
    sin_part = (jnp.sin(theta) * scale).astype(BF16).reshape(N_TILE, P_HERE, A)
    first = jnp.concatenate([cos_part, sin_part], axis=2)
    second = jnp.concatenate([-sin_part, cos_part], axis=2)
    full = jnp.stack([first, second], axis=1).reshape(2 * P_G, 2 * A)
    w_ref[...] = full.T.astype(F32)
    half_rows(w_ref, weights_ref, mine)
    low = mine * (A - HALF)
    near = [
        band_t(interp_ref, offsets_ref, 0, mine, mine, low, HALF),
        band_t(interp_ref, offsets_ref, 0, mine, 1 - mine, low, HALF),
    ]
    near = jnp.concatenate(near, axis=0)
    nt = (((1,), (1,)), ((), ()))
    near_ref[...] = lax.dot_general(pick_ref[...], near, nt, preferred_element_type=F32).astype(BF16)


def half_rows(full_ref, out_ref, mine):
    rows = []
    for side in (1 - mine, mine):
        for part in range(2):
            low = pl.multiple_of(part * A + side * (A - HALF), 8)
            rows.append(full_ref[pl.ds(low, HALF), :])
    out_ref[...] = jnp.concatenate(rows, axis=0).astype(BF16)


def project_kernel(weights_ref, got_ref, out_ref, *, first):
    weights = weights_ref[first : first + 2 * HALF, :]
    for j in range(PER):
        block = got_ref[:, 32 * j : 32 * j + 32, :].reshape(2 * P_G, KTAP)
        made = jnp.dot(weights, block, preferred_element_type=F32).astype(BF16)
        out_ref[:, 128 * j : 128 * j + 128] = made


def own_kernel(after_ref, weights_ref, got_ref, out_ref):
    del after_ref
    project_kernel(weights_ref, got_ref, out_ref, first=2 * HALF)


def far_kernel(after_ref, interp_ref, offsets_ref, far_ref, full_ref):
    del after_ref
    y = lax.axis_index("y")
    bits = [y & 1, y >> 1 & 1, y >> 2 & 1]
    low = jnp.int32(0)
    for bit in reversed(bits):
        low = jnp.clip((bit * A + low) // 2 - KB // 2, 0, A - KB)
    n = lax.broadcasted_iota(jnp.int32, (FAR_ROWS, A), 0)
    second = n >= WIN
    rows = low + n - jnp.where(second, WIN, 0)
    chain = []
    for q in range(2):
        real, imag = band_parts(interp_ref, offsets_ref, 1, bits[0], q, rows)
        left = jnp.where(second, -imag, real)
        right = jnp.where(second, real, imag)
        chain.append(jnp.concatenate([left, right], axis=1))
    chain = jnp.concatenate(chain, axis=0)
    for level in range(2, 4):
        grown = []
        for q in range(2):
            step = band_t(interp_ref, offsets_ref, level, bits[level - 1], q, 0, A)
            grown.append(jnp.dot(chain.astype(BF16), step, preferred_element_type=F32))
        chain = jnp.concatenate(grown, axis=0)
    chain = chain.reshape(N_Y, FAR_ROWS, 2 * A)
    first = chain[:, :MAIN].reshape(N_Y * MAIN, 2 * A)
    rest = chain[:, MAIN:].reshape(N_Y * 8, 2 * A)
    full_ref[...] = jnp.concatenate([first, rest], axis=0).T
    half_rows(full_ref, far_ref, lax.axis_index("h"))


def last_kernel(after_ref, interp_ref, offsets_ref, last_ref):
    del after_ref
    mine = lax.axis_index("h")
    low = mine * (A - HALF)
    last = [
        band_t(interp_ref, offsets_ref, 4, mine, mine, low, HALF),
        band_t(interp_ref, offsets_ref, 4, mine, 1 - mine, low, HALF),
    ]
    last_ref[...] = jnp.concatenate(last, axis=0).T


def merge_kernel(after_ref, near_ref, own_ref, other_ref, out_ref):
    del after_ref
    size = N_Y * PER * REST
    order = one_hot(size, size, lambda r, c: c == r // 4 % 4 * (N_Y * REST) + r // 16 * 4 + r % 4)
    data = jnp.concatenate([own_ref[...], other_ref[...]], axis=0)
    made = jnp.dot(near_ref[...], data, preferred_element_type=F32)
    made = made.astype(BF16)
    for y in range(N_Y):
        for j in range(PER):
            out_ref[y, MAIN * j : MAIN * j + MAIN] = made[MAIN * y : MAIN * y + MAIN, 128 * j : 128 * j + 128]
    rest = made[N_Y * MAIN :]
    rest = jnp.concatenate([rest[:, 128 * j : 128 * j + 128] for j in range(PER)], axis=0)
    rest = jnp.dot(order, rest, preferred_element_type=F32).astype(BF16)
    for y in range(N_Y):
        out_ref[y, PER * MAIN :] = rest[16 * y : 16 * y + 16]


def join_kernel(far_ref, got_ref, send_ref, own_ref):
    order = one_hot(
        PER * N_Y * 8,
        N_Y * 16,
        lambda r, c: (c == r // 8 % N_Y * 16 + r // (8 * N_Y) * 4 + r % 8) & (r % 8 < REST),
    )
    rest = got_ref[:, PER * MAIN :, :].reshape(N_Y * 16, KTAP)
    rest = jnp.dot(order, rest, preferred_element_type=F32).astype(BF16)
    for j in range(PER):
        block = got_ref[:, MAIN * j : MAIN * j + MAIN, :].reshape(N_Y * MAIN, KTAP)
        block = jnp.concatenate([block, rest[8 * N_Y * j : 8 * N_Y * (j + 1)]], axis=0)
        made = jnp.dot(far_ref[...], block, preferred_element_type=F32).astype(BF16)
        send_ref[:, 128 * j : 128 * j + 128] = made[: 2 * HALF]
        own_ref[:, 128 * j : 128 * j + 128] = made[2 * HALF :]


def final_kernel(last_ref, own_ref, other_ref, out_ref):
    data = jnp.concatenate([own_ref[...], other_ref[...]], axis=0)
    made = jnp.dot(last_ref[...], data, preferred_element_type=F32).astype(BF16)
    out_ref[0] = made[:A]
    out_ref[1] = made[A:]


def call(body, ins, outs, scratch=(), limit=48):
    return pl.pallas_call(
        body,
        out_shape=[jax.ShapeDtypeStruct(shape, BF16) for shape in outs],
        in_specs=ins,
        out_specs=[VMEM] * len(outs),
        scratch_shapes=list(scratch),
        compiler_params=pltpu.CompilerParams(vmem_limit_bytes=limit * 2**20),
    )


def run_compress(owner, chirp, x):
    return call(
        compress_kernel,
        [HBM] * 3,
        [(N_TILE, PER, 2, P_HERE, KTAP), (16, KTAP)],
        [
            pltpu.SMEM((N_TILE,), jnp.int32),
            pltpu.VMEM((CH, 2, KTAP), BF16),
            pltpu.VMEM((P_HERE, CH, 2 * BLOCKS, KTAP), BF16),
            pltpu.SMEM((N_TILE,), jnp.int32),
            pltpu.VMEM((4 * CH * KTAP, 2 * KTAP), BF16),
            pltpu.VMEM(((BLOCKS + 1) * P_HERE, 2 * CH * KTAP), BF16),
            pltpu.SemaphoreType.DMA((BLOCKS // 8 + 2,)),
        ],
        limit=60,
    )(owner, chirp, x)


def shards(raw, chirp, steer, offsets, interp, owner):
    x = raw.reshape(P_HERE, CH, 2, BLOCKS, KTAP).transpose(0, 1, 3, 2, 4)
    x = x.reshape(P_HERE, CH, 2 * BLOCKS, KTAP)
    packed, token = run_compress(owner, chirp, x)
    packed = packed.reshape(N_TILE, PER * 2 * P_HERE, KTAP)
    got = lax.all_to_all(packed, ("x", "l"), 0, 0, tiled=True)
    weights, near = call(
        prep_kernel,
        [VMEM] * 5,
        [(4 * HALF, 2 * P_G), (N_Y * (MAIN + REST), 4 * HALF)],
        [pltpu.VMEM((2 * A, 2 * P_G), F32)],
    )(token, steer, interp, offsets, jnp.asarray(row_pick()))
    send_rows = functools.partial(project_kernel, first=0)
    (send,) = call(send_rows, [VMEM] * 2, [(2 * HALF, R)])(weights, got)
    other = lax.ppermute(send, "c", [(0, 1), (1, 0)])
    (own,) = call(own_kernel, [VMEM] * 3, [(2 * HALF, R)])(send, weights, got)
    (far,) = call(
        far_kernel,
        [VMEM] * 3,
        [(4 * HALF, N_Y * FAR_ROWS)],
        [pltpu.VMEM((2 * A, N_Y * FAR_ROWS), F32)],
    )(own, interp, offsets)
    (pieces,) = call(merge_kernel, [VMEM] * 4, [(N_Y, PIECE, KTAP)])(far, near, own, other)
    parts = lax.all_to_all(pieces, "y", 0, 0, tiled=True)
    send, own = call(join_kernel, [VMEM] * 2, [(2 * HALF, R)] * 2)(far, parts)
    other = lax.ppermute(send, "h", [(0, 1), (1, 0)])
    (last,) = call(last_kernel, [VMEM] * 3, [(2 * A, 4 * HALF)])(own, interp, offsets)
    (image,) = call(final_kernel, [VMEM] * 3, [(2, A, R)])(last, own, other)
    return image


def solution(mesh):
    split = Mesh(mesh.devices.reshape(2, 8, 2, 4, 4), ("h", "y", "c", "x", "l"))
    pulse = ("h", "y", "c")
    tile = ("x", "l")
    placed = (P(pulse + tile, None, None, None), P(), P(pulse, None), P(), P(), P())
    return jax.shard_map(
        shards, mesh=split, in_specs=placed, out_specs=P(None, pulse, tile), check_vma=False
    )
```
